128 devices in a mesh: dp: 32 (over y, x, core), tensor: 4 (over z).
Axes of the slice: x: 4, y: 4, z: 4, core: 2. Of those that a mesh axis runs over, the one named last changes fastest.
Arguments:
- tokens: bfloat16 [6, 16384, 4096], P(None, 'dp', 'tensor'), may hold values from -16 to 16
- router: bfloat16 [16, 4096], P(None, 'tensor'), may hold values from -32 to 32
- w_gate: bfloat16 [4, 14336, 4096], P('tensor', 'dp'), may hold values from -0.625 to 0.625
- w_up: bfloat16 [4, 14336, 4096], P('tensor', 'dp'), may hold values from -0.625 to 0.625
- w_down: bfloat16 [4, 14336, 4096], P('tensor', 'dp'), may hold values from -0.046875 to 0.046875
Outputs:
- mixed: bfloat16 [6, 16384, 4096], P(None, 'dp', 'tensor')
- log_total: float32 [6, 16384], P(None, 'dp')
The draws below stay inside these ranges and needn't reach their ends.
All inputs are finite; a program needn't handle non-finite values.
Results may differ from the reference program's by a relative error of at most 0.0096.
Values may be sent and summed in bfloat16 or wider, within the bound.
No kernel may reach another device: no remote copies, remote signals or barrier semaphores. Data moves between devices by JAX's collectives and lax.ppermute only.
A program may use at most 128 MiB of HBM per device.

```python
import math
import jax
import jax.numpy as jnp
from jax import lax

D = 4096
FF = 14336
SLOTS = 4
GROUPS = 6
EW = 4
WS = 16
TOKENS = 16384


def shared_base(key):
    return jnp.clip(jax.random.normal(key, (WS, D), jnp.float32), -5.0, 5.0)


def draw_tokens(key, part):
    key = jax.random.fold_in(key, 11)
    first_key = jax.random.fold_in(key, 0)
    position = jnp.arange(D, dtype=jnp.float32)
    rising = jnp.exp(0.5 * math.log(3.0) * position / max(D - 1, 1))
    normals = jax.random.normal(first_key, (GROUPS, TOKENS, D), jnp.float32)
    values = jnp.clip(normals * rising, -16.0, 16.0)
    return values.astype(jnp.bfloat16)


def draw_router(key, part):
    anchors = shared_base(key)
    key = jax.random.fold_in(key, 23)
    first_key = jax.random.fold_in(key, 0)
    spread = jnp.exp(jax.random.uniform(first_key, (WS, 1), jnp.float32, math.log(4.0), math.log(5.0)))
    router_rows = anchors * spread / math.sqrt(D)
    return jnp.clip(router_rows, -32.0, 32.0).astype(jnp.bfloat16)


def shard_levels(rng, shape, cuts, smallest, top_value):
    factor_of, own = 1.0, jax.random.fold_in(rng, 6)
    for axis_at, blocks in cuts:
        steps = jnp.exp(jax.random.uniform(jax.random.fold_in(own, axis_at), (blocks,), jnp.float32, smallest / len(cuts), top_value / len(cuts)))
        factor_of = factor_of * jnp.repeat(steps, shape[axis_at] // blocks).reshape([-1 if axis == axis_at else 1 for axis in range(len(shape))])
    return factor_of


def normal_values(rng, shape, scale, limit, cuts=(), kind=jnp.bfloat16):
    factor_of = shard_levels(rng, shape, cuts, -0.22, 0.18) if cuts else 1.0
    entries = jax.random.normal(rng, shape, jnp.float32) * scale * factor_of
    return jnp.minimum(jnp.maximum(entries, -limit), limit).astype(kind)


def setup_inputs(seed: int = 0) -> dict:
    splits = jax.random.split(jax.random.key(seed), 6)
    return {
        "tokens": draw_tokens(jax.random.fold_in(splits[5], 71), 0),
        "router": draw_router(jax.random.fold_in(splits[5], 71), 0),
        "w_gate": normal_values(splits[2], (EW, FF, D), (D // 48) ** -0.5, 0.625, ((0, 4), (1, 32))),
        "w_up": normal_values(splits[3], (EW, FF, D), (D // 48) ** -0.5, 0.625, ((0, 4), (1, 32))),
        "w_down": normal_values(splits[4], (EW, FF, D), FF ** -0.5, 0.046875, ((0, 4), (1, 32))),
    }


epsilon = 1e-05

def front_group(group_rows, router):
    as_float = group_rows.astype(jnp.float32)
    norm_scale = lax.rsqrt(lax.optimization_barrier(jnp.mean(as_float * as_float, axis=1)) + epsilon)
    logits = jnp.dot(router, group_rows.T, preferred_element_type=jnp.float32) * norm_scale[None, :]
    column_peak = lax.optimization_barrier(jnp.max(logits, axis=1, keepdims=True))
    powers = jnp.exp(logits - column_peak)
    column_sum = lax.optimization_barrier(jnp.sum(powers, axis=1, keepdims=True))
    weights = (powers * norm_scale[None, :]).astype(jnp.bfloat16)
    slot_in = (jnp.dot(weights, group_rows, preferred_element_type=jnp.float32) / column_sum).astype(jnp.bfloat16)
    row_peak = lax.optimization_barrier(jnp.max(logits, axis=0, keepdims=True))
    row_powers = jnp.exp(logits - row_peak)
    row_sum = lax.optimization_barrier(jnp.sum(row_powers, axis=0, keepdims=True))
    combine = (row_powers / row_sum).astype(jnp.bfloat16)
    log_total = (row_peak + jnp.log(row_sum))[0]
    return (slot_in, combine, log_total)

def mix_group(paired):
    combine, slot_out = paired
    return jnp.dot(combine.T, slot_out, preferred_element_type=jnp.float32).astype(jnp.bfloat16)

def reference(tokens, router, w_gate, w_up, w_down):
    slot_in, combine, log_total = lax.map(lambda group_rows: front_group(group_rows, router), tokens)
    groups = tokens.shape[0]
    results = []
    for expert in range(w_gate.shape[0]):
        slot_rows = slot_in[:, expert * SLOTS:(expert + 1) * SLOTS, :].reshape(groups * SLOTS, D)
        gate_act = jnp.dot(slot_rows, w_gate[expert].T, preferred_element_type=jnp.float32)
        up_act = jnp.dot(slot_rows, w_up[expert].T, preferred_element_type=jnp.float32)
        hidden = (jax.nn.silu(gate_act) * up_act).astype(jnp.bfloat16)
        expert_out = jnp.dot(hidden, w_down[expert], preferred_element_type=jnp.float32).astype(jnp.bfloat16)
        results.append(expert_out.reshape(groups, SLOTS, D))
    slot_out = jnp.concatenate(results, axis=1)
    mixed = lax.map(mix_group, (combine, slot_out))
    return (mixed, log_total)
```

```python
import functools

import jax
import jax.numpy as jnp
from jax import lax
from jax.experimental import pallas as pl
from jax.experimental.pallas import tpu as pltpu
from jax.sharding import PartitionSpec as P

GROUPS = 6
SLOTS = 4
EXPERTS = 4
WS = SLOTS * EXPERTS
PAD = 8
LANES = 128
TILES = 8
TOK = 512
WIDTH = TILES * LANES
FULL = 4096
HID = 448
HALF = GROUPS // 2
LROWS = HALF * WS + PAD

epsilon = 1e-05
bf16 = jnp.bfloat16
f32 = jnp.float32
NT = (((1,), (1,)), ((), ()))
VM = pl.BlockSpec(memory_space=pltpu.VMEM)


def params(mib):
    return pltpu.CompilerParams(vmem_limit_bytes=mib << 20)


def logits_kernel(tokens_ref, router_ref, out_ref):
    step = pl.program_id(0)
    tok = tokens_ref[0]
    out_ref[pl.ds(pl.multiple_of(step * WS, WS), WS), :] = lax.dot_general(
        router_ref[...], tok, NT, preferred_element_type=f32
    )
    total = jnp.zeros((TOK, LANES), f32)
    for t in range(TILES):
        part = tok[:, t * LANES:(t + 1) * LANES].astype(f32)
        total += part * part
    row = lax.dot_general(
        jnp.ones((PAD, LANES), f32), total, NT,
        precision=lax.Precision.HIGHEST, preferred_element_type=f32,
    )

    @pl.when(step == 0)
    def _():
        out_ref[HALF * WS:, :] = jnp.zeros((PAD, TOK), f32)

    out_ref[pl.ds(HALF * WS + step, 1), :] = row[0:1]


def partial_logits(tokens, router, half):
    return pl.pallas_call(
        logits_kernel,
        grid=(HALF,),
        in_specs=[
            pl.BlockSpec((1, TOK, WIDTH), lambda g: (half * HALF + g, 0, 0)),
            pl.BlockSpec((WS, WIDTH), lambda g: (0, 0)),
        ],
        out_specs=pl.BlockSpec((LROWS, TOK), lambda g: (0, 0)),
        out_shape=jax.ShapeDtypeStruct((LROWS, TOK), f32),
        compiler_params=params(16),
        name="partial_logits",
    )(tokens, router)


def split3(value):
    high = value.astype(bf16).astype(f32)
    rest = value - high
    mid = rest.astype(bf16).astype(f32)
    return high, mid, rest - mid


def spread_rows(ref, rows, value):
    for n in range(TOK // LANES):
        ref[n, rows, :] = value[:, n * LANES:(n + 1) * LANES]


def dispatch_kernel(*refs):
    parts, (tokens_ref, send_ref, combine_ref, log_ref, wts, cmb, peaks, sums) = refs[:8], refs[8:]
    wts[...] = jnp.zeros_like(wts)
    cmb[...] = jnp.zeros_like(cmb)
    peaks[...] = jnp.zeros_like(peaks)
    sums[...] = jnp.zeros_like(sums)
    for half in range(2):
        a, b, c, d = (ref[...] for ref in parts[half * 4:half * 4 + 4])
        total = (a + b) + (c + d)
        squares = total[HALF * WS:]
        scale = lax.rsqrt(squares * (1.0 / FULL) + epsilon)
        for h in range(HALF):
            g = half * HALF + h
            rows = pl.ds(g, WS, stride=PAD)
            norm = scale[h:h + 1]
            logits = total[h * WS:(h + 1) * WS] * norm
            peak = jnp.max(logits, axis=1, keepdims=True)
            powers = jnp.exp(logits - peak)
            spread_rows(wts, rows, powers * norm)
            peaks[rows, :] = jnp.broadcast_to(peak, (WS, LANES))
            sums[rows, :] = jnp.broadcast_to(jnp.sum(powers, axis=1, keepdims=True), (WS, LANES))
            row_peak = jnp.max(logits, axis=0, keepdims=True)
            row_powers = jnp.exp(logits - row_peak)
            row_sum = jnp.sum(row_powers, axis=0, keepdims=True)
            spread_rows(cmb, rows, row_powers / row_sum)
            log_ref[g:g + 1, :] = row_peak + jnp.log(row_sum)
    combine = jnp.concatenate([cmb[n] for n in range(TOK // LANES)], axis=1)
    combine_ref[...] = jnp.concatenate(
        [combine[(4 * k + s) * PAD:(4 * k + s + 1) * PAD] for s in range(SLOTS) for k in range(EXPERTS)]
    ).astype(bf16)
    weights = jnp.concatenate([wts[n] for n in range(TOK // LANES)], axis=1).astype(bf16)
    group = lax.broadcasted_iota(jnp.int32, (WS * PAD, TOK), 0) % PAD
    acc = jnp.zeros((WS * PAD, WIDTH), f32)
    for g in range(GROUPS):
        mine = jnp.where(group == g, weights, jnp.zeros_like(weights))
        acc += jnp.dot(mine, tokens_ref[g], preferred_element_type=f32)
    lane = lax.broadcasted_iota(jnp.int32, (WS * PAD, LANES), 1)
    member = lax.broadcasted_iota(jnp.int32, (WS * PAD, LANES), 0) % PAD
    meta = jnp.zeros((WS * PAD, LANES), f32)
    for n, value in enumerate(split3(peaks[...]) + split3(sums[...])):
        meta += jnp.where(lane == member + n * PAD, value, 0.0)
    meta = jnp.sum(meta.reshape(WS, PAD, LANES), axis=1, keepdims=True)
    meta = jnp.broadcast_to(meta, (WS, PAD, LANES)).reshape(WS * PAD, LANES)
    for t in range(TILES):
        tile = jnp.where(member == GROUPS, meta, acc[:, t * LANES:(t + 1) * LANES])
        for s in range(SLOTS):
            block = jnp.concatenate(
                [tile[(4 * k + s) * PAD:(4 * k + s + 1) * PAD] for k in range(EXPERTS)]
            )
            send_ref[pl.ds((s * TILES + t) * EXPERTS * PAD, EXPERTS * PAD), :] = block.astype(bf16)


def dispatch(parts, tokens):
    return pl.pallas_call(
        dispatch_kernel,
        in_specs=[VM] * 9,
        out_specs=[VM] * 3,
        out_shape=[
            jax.ShapeDtypeStruct((SLOTS * TILES * EXPERTS * PAD, LANES), bf16),
            jax.ShapeDtypeStruct((WS * PAD, TOK), bf16),
            jax.ShapeDtypeStruct((GROUPS, TOK), f32),
        ],
        scratch_shapes=[
            pltpu.VMEM((TOK // LANES, WS * PAD, LANES), f32),
            pltpu.VMEM((TOK // LANES, WS * PAD, LANES), f32),
            pltpu.VMEM((WS * PAD, LANES), f32),
            pltpu.VMEM((WS * PAD, LANES), f32),
        ],
        compiler_params=params(20),
        name="dispatch",
    )(*parts, tokens)


def merge_kernel(got_ref, out_ref, wide):
    wide[...] = got_ref[...].astype(f32)
    meta = wide[pl.ds(GROUPS, 32, stride=EXPERTS * PAD), :]
    shift = lambda n: pltpu.roll(meta, (LANES - n * PAD) % LANES, 1)
    lane = lax.broadcasted_iota(jnp.int32, (32, LANES), 1)
    peak = (meta + shift(1)) + shift(2)
    local = (shift(3) + shift(4)) + shift(5)
    peak = jnp.where(lane < GROUPS, peak, 0.0)
    factor = jnp.exp(peak - jnp.max(peak, axis=0, keepdims=True))
    total = jnp.sum(factor * local, axis=0, keepdims=True)
    factor = jnp.where(lane < GROUPS, factor / jnp.where(lane[0:1] < GROUPS, total, 1.0), 0.0)
    square = jnp.concatenate([factor, jnp.zeros((LANES - 32, LANES), f32)])
    columns = square.T[0:PAD]
    acc = [jnp.zeros((PAD, LANES), f32) for _ in range(4)]
    for i in range(32):
        by = jnp.broadcast_to(columns[:, i:i + 1], (PAD, LANES))
        for z in range(4):
            row = (i * 4 + z) * PAD
            acc[z] += by * wide[row:row + PAD, :]
    block = jnp.concatenate(acc).astype(bf16)
    for i in range(32):
        out_ref[i] = block


def add_kernel(got_ref, out_ref):
    rows = 4 * PAD
    acc = got_ref[0:rows, :].astype(f32)
    for i in range(1, 32):
        acc += got_ref[i * rows:(i + 1) * rows, :].astype(f32)
    block = acc.astype(bf16)
    for i in range(32):
        out_ref[i] = block


def merge(got):
    return pl.pallas_call(
        merge_kernel,
        in_specs=[VM],
        out_specs=VM,
        out_shape=jax.ShapeDtypeStruct((32, 4 * PAD, LANES), bf16),
        scratch_shapes=[pltpu.VMEM((32 * 4 * PAD, LANES), f32)],
        compiler_params=params(8),
        name="merge",
    )(got)


def add_up(got):
    return pl.pallas_call(
        add_kernel,
        in_specs=[VM],
        out_specs=VM,
        out_shape=jax.ShapeDtypeStruct((32, 4 * PAD, LANES), bf16),
        compiler_params=params(8),
        name="add_up",
    )(got)


def expert_kernel(got_ref, gate_ref, up_ref, down_ref, send_ref, rows):
    for s in range(SLOTS):
        for t in range(TILES):
            block = got_ref[s * TILES + t].astype(f32)
            for z in range(4):
                at = (z * TILES + t) * LANES
                rows[s * PAD:(s + 1) * PAD, at:at + LANES] = block[z * PAD:(z + 1) * PAD]
    slot_in = rows[...].astype(bf16)
    gate = lax.dot_general(slot_in, gate_ref[0], NT, preferred_element_type=f32)
    up = lax.dot_general(slot_in, up_ref[0], NT, preferred_element_type=f32)
    hidden = (gate / (1.0 + jnp.exp(-gate)) * up).astype(bf16)
    out = jnp.dot(hidden, down_ref[0], preferred_element_type=f32)
    for s in range(SLOTS):
        for t in range(TILES):
            block = jnp.concatenate(
                [
                    out[s * PAD:(s + 1) * PAD, (z * TILES + t) * LANES:(z * TILES + t + 1) * LANES]
                    for z in range(4)
                ]
            )
            send_ref[pl.ds((s * TILES + t) * 4 * PAD, 4 * PAD), :] = block.astype(bf16)


def expert(got, w_gate, w_up, w_down):
    return pl.pallas_call(
        expert_kernel,
        in_specs=[VM] * 4,
        out_specs=VM,
        out_shape=jax.ShapeDtypeStruct((SLOTS * TILES * 4 * PAD, LANES), bf16),
        scratch_shapes=[pltpu.VMEM((SLOTS * PAD, FULL), f32)],
        compiler_params=params(24),
        name="expert",
    )(got, w_gate, w_up, w_down)


def mix_kernel(got_ref, combine_ref, out_ref, slots, turned):
    step = pl.program_id(0)

    @pl.when(step == 0)
    def _():
        for s in range(SLOTS):
            for t in range(TILES):
                slots[s * 32:(s + 1) * 32, t * LANES:(t + 1) * LANES] = got_ref[s * TILES + t]
        turned[...] = combine_ref[...].astype(f32).T

    lane = lax.broadcasted_iota(jnp.int32, (TOK, WS * PAD), 1) % PAD
    mine = jnp.where(lane == step, turned[...], 0.0).astype(bf16)
    out_ref[0] = jnp.dot(mine, slots[...], preferred_element_type=f32).astype(bf16)


def mix(got, combine):
    return pl.pallas_call(
        mix_kernel,
        grid=(GROUPS,),
        in_specs=[
            pl.BlockSpec((32, 4 * PAD, LANES), lambda g: (0, 0, 0)),
            pl.BlockSpec((WS * PAD, TOK), lambda g: (0, 0)),
        ],
        out_specs=pl.BlockSpec((1, TOK, WIDTH), lambda g: (g, 0, 0)),
        out_shape=jax.ShapeDtypeStruct((GROUPS, TOK, WIDTH), bf16),
        scratch_shapes=[
            pltpu.VMEM((WS * PAD, WIDTH), bf16),
            pltpu.VMEM((TOK, WS * PAD), f32),
        ],
        compiler_params=params(20),
        name="mix",
    )(got, combine)


def everyone(x):
    x = x.reshape(128, PAD, LANES)
    x = lax.all_to_all(x, ("dp", "tensor"), 0, 0, tiled=True)
    return x.reshape(128 * PAD, LANES)


def per_device(tokens, router, w_gate, w_up, w_down):
    parts = []
    for half in range(2):
        own = partial_logits(tokens, router, half)
        parts.append(own)
        for k in range(1, 4):
            parts.append(lax.ppermute(own, "tensor", [(i, (i + k) % 4) for i in range(4)]))
    send, combine, log_total = dispatch(parts, tokens)
    spread = merge(everyone(send))
    slot_in = lax.all_to_all(spread, "dp", 0, 0, tiled=True)
    outs = expert(slot_in, w_gate, w_up, w_down)
    spread = add_up(everyone(outs))
    slot_out = lax.all_to_all(spread, "dp", 0, 0, tiled=True)
    return (mix(slot_out, combine), log_total)


def solution(mesh):
    in_specs = (
        P(None, "dp", "tensor"),
        P(None, "tensor"),
        P("tensor", "dp", None),
        P("tensor", "dp", None),
        P("tensor", "dp", None),
    )
    out_specs = (P(None, "dp", "tensor"), P(None, "dp"))
    return jax.shard_map(
        per_device, mesh=mesh, in_specs=in_specs, out_specs=out_specs, check_vma=False
    )
```

```python
import functools

import jax
import jax.numpy as jnp
from jax import lax
from jax.experimental import pallas as pl
from jax.experimental.pallas import tpu as pltpu
from jax.sharding import PartitionSpec as P

GROUPS = 6
SLOTS = 4
EXPERTS = 4
WS = SLOTS * EXPERTS
PAD = 8
LANES = 128
TILES = 8
TOK = 512
WIDTH = TILES * LANES
FULL = 4096
HID = 448
HALF = GROUPS // 2
LROWS = HALF * WS + PAD

CHUNK = 256

epsilon = 1e-05
bf16 = jnp.bfloat16
f32 = jnp.float32
NT = (((1,), (1,)), ((), ()))
VM = pl.BlockSpec(memory_space=pltpu.VMEM)
HBM = pl.BlockSpec(memory_space=pltpu.HBM)


def params(mib):
    return pltpu.CompilerParams(vmem_limit_bytes=mib << 20)


def logits_kernel(tokens_ref, router_ref, first_ref, second_ref, held_a, held_b, router, arrived):
    held = [(held_a, held_b)[g // HALF].at[g % HALF] for g in range(GROUPS)]
    fetch = pltpu.make_async_copy(router_ref, router, arrived.at[GROUPS])
    fetch.start()
    copies = [
        pltpu.make_async_copy(tokens_ref.at[g], held[g], arrived.at[g]) for g in range(GROUPS)
    ]
    for copy in copies:
        copy.start()
    fetch.wait()
    for g in range(GROUPS):
        out_ref, h = (first_ref, second_ref)[g // HALF], g % HALF
        if h == 0:
            out_ref[HALF * WS:, :] = jnp.zeros((PAD, TOK), f32)
        copies[g].wait()
        tok = held[g][...]
        out_ref[h * WS:(h + 1) * WS, :] = lax.dot_general(
            router[...], tok, NT, preferred_element_type=f32
        )
        total = jnp.zeros((TOK, LANES), f32)
        for t in range(TILES):
            part = tok[:, t * LANES:(t + 1) * LANES].astype(f32)
            total += part * part
        out_ref[HALF * WS + h:HALF * WS + h + 1, :] = jnp.sum(total.T, axis=0, keepdims=True)


def partial_logits(tokens, router):
    logits = jax.ShapeDtypeStruct((LROWS, TOK), f32)
    held = jax.ShapeDtypeStruct((HALF, TOK, WIDTH), tokens.dtype)
    return pl.pallas_call(
        logits_kernel,
        in_specs=[HBM, HBM],
        out_specs=[VM] * 4,
        out_shape=[logits, logits, held, held],
        scratch_shapes=[
            pltpu.VMEM(router.shape, router.dtype),
            pltpu.SemaphoreType.DMA((GROUPS + 1,)),
        ],
        compiler_params=params(46),
        name="partial_logits",
    )(tokens, router)


def split3(value):
    high = value.astype(bf16).astype(f32)
    rest = value - high
    mid = rest.astype(bf16).astype(f32)
    return high, mid, rest - mid


def spread_rows(ref, rows, value):
    for n in range(TOK // LANES):
        ref[n, rows, :] = value[:, n * LANES:(n + 1) * LANES]


def dispatch_kernel(*refs):
    parts, (held_a, held_b, send_ref, combine_ref, log_ref, wts, cmb, peaks, sums) = refs[:4], refs[4:]
    wts[...] = jnp.zeros_like(wts)
    cmb[...] = jnp.zeros_like(cmb)
    peaks[...] = jnp.zeros_like(peaks)
    sums[...] = jnp.zeros_like(sums)
    totals = [parts[0][...] + parts[1][...], parts[2][...] + parts[3][...]]
    scales = [lax.rsqrt(total[HALF * WS:] * (1.0 / FULL) + epsilon) for total in totals]
    for g in range(GROUPS):
        half, h = divmod(g, HALF)
        rows = pl.ds(g, WS, stride=PAD)
        norm = scales[half][h:h + 1]
        logits = totals[half][h * WS:(h + 1) * WS] * norm
        peak = jnp.max(logits, axis=1, keepdims=True)
        powers = jnp.exp(logits - peak)
        spread_rows(wts, rows, powers * norm)
        peaks[rows, :] = jnp.broadcast_to(peak, (WS, LANES))
        sums[rows, :] = jnp.broadcast_to(jnp.sum(powers, axis=1, keepdims=True), (WS, LANES))
        row_peak = jnp.max(logits, axis=0, keepdims=True)
        row_powers = jnp.exp(logits - row_peak)
        row_sum = jnp.sum(row_powers, axis=0, keepdims=True)
        spread_rows(cmb, rows, row_powers / row_sum)
        log_ref[g:g + 1, :] = row_peak + jnp.log(row_sum)
    combine = jnp.concatenate([cmb[n] for n in range(TOK // LANES)], axis=1)
    combine_ref[...] = jnp.concatenate(
        [combine[(4 * k + s) * PAD:(4 * k + s + 1) * PAD] for s in range(SLOTS) for k in range(EXPERTS)]
    ).astype(bf16)
    weights = jnp.concatenate([wts[n] for n in range(TOK // LANES)], axis=1).astype(bf16)
    group = lax.broadcasted_iota(jnp.int32, (WS * PAD, TOK), 0) % PAD
    acc = jnp.zeros((WS * PAD, WIDTH), f32)
    for g in range(GROUPS):
        mine = jnp.where(group == g, weights, jnp.zeros_like(weights))
        held = (held_a, held_b)[g // HALF]
        acc += jnp.dot(mine, held[g % HALF], preferred_element_type=f32)
    lane = lax.broadcasted_iota(jnp.int32, (WS * PAD, LANES), 1)
    member = lax.broadcasted_iota(jnp.int32, (WS * PAD, LANES), 0) % PAD
    meta = jnp.zeros((WS * PAD, LANES), f32)
    for n, value in enumerate(split3(peaks[...]) + split3(sums[...])):
        meta += jnp.where(lane == member + n * PAD, value, 0.0)
    meta = jnp.sum(meta.reshape(WS, PAD, LANES), axis=1, keepdims=True)
    meta = jnp.broadcast_to(meta, (WS, PAD, LANES)).reshape(WS * PAD, LANES)
    for t in range(TILES):
        tile = jnp.where(member == GROUPS, meta, acc[:, t * LANES:(t + 1) * LANES])
        for s in range(SLOTS):
            block = jnp.concatenate(
                [tile[(4 * k + s) * PAD:(4 * k + s + 1) * PAD] for k in range(EXPERTS)]
            )
            send_ref[pl.ds((s * TILES + t) * EXPERTS * PAD, EXPERTS * PAD), :] = block.astype(bf16)


def dispatch(parts, held):
    return pl.pallas_call(
        dispatch_kernel,
        in_specs=[VM] * 6,
        out_specs=[VM] * 3,
        out_shape=[
            jax.ShapeDtypeStruct((SLOTS * TILES * EXPERTS * PAD, LANES), bf16),
            jax.ShapeDtypeStruct((WS * PAD, TOK), bf16),
            jax.ShapeDtypeStruct((GROUPS, TOK), f32),
        ],
        scratch_shapes=[
            pltpu.VMEM((TOK // LANES, WS * PAD, LANES), f32),
            pltpu.VMEM((TOK // LANES, WS * PAD, LANES), f32),
            pltpu.VMEM((WS * PAD, LANES), f32),
            pltpu.VMEM((WS * PAD, LANES), f32),
        ],
        compiler_params=params(20),
        name="dispatch",
    )(*parts, *held)


def merge_kernel(got_ref, out_ref, wide):
    wide[...] = got_ref[...].astype(f32)
    meta = wide[pl.ds(GROUPS, 32, stride=EXPERTS * PAD), :]
    shift = lambda n: pltpu.roll(meta, (LANES - n * PAD) % LANES, 1)
    lane = lax.broadcasted_iota(jnp.int32, (32, LANES), 1)
    peak = (meta + shift(1)) + shift(2)
    local = (shift(3) + shift(4)) + shift(5)
    peak = jnp.where(lane < GROUPS, peak, 0.0)
    factor = jnp.exp(peak - jnp.max(peak, axis=0, keepdims=True))
    total = jnp.sum(factor * local, axis=0, keepdims=True)
    factor = jnp.where(lane < GROUPS, factor / jnp.where(lane[0:1] < GROUPS, total, 1.0), 0.0)
    square = jnp.concatenate([factor, jnp.zeros((LANES - 32, LANES), f32)])
    columns = square.T[0:PAD]
    acc = [jnp.zeros((PAD, LANES), f32) for _ in range(4)]
    for i in range(32):
        by = jnp.broadcast_to(columns[:, i:i + 1], (PAD, LANES))
        for z in range(4):
            row = (i * 4 + z) * PAD
            acc[z] += by * wide[row:row + PAD, :]
    block = jnp.concatenate(acc).astype(bf16)
    for i in range(32):
        out_ref[i] = block


def add_kernel(got_ref, out_ref):
    rows = 4 * PAD
    acc = got_ref[0:rows, :].astype(f32)
    for i in range(1, 32):
        acc += got_ref[i * rows:(i + 1) * rows, :].astype(f32)
    block = acc.astype(bf16)
    for i in range(32):
        out_ref[i] = block


def merge(got):
    return pl.pallas_call(
        merge_kernel,
        in_specs=[VM],
        out_specs=VM,
        out_shape=jax.ShapeDtypeStruct((32, 4 * PAD, LANES), bf16),
        scratch_shapes=[pltpu.VMEM((32 * 4 * PAD, LANES), f32)],
        compiler_params=params(8),
        name="merge",
    )(got)


def add_up(got):
    return pl.pallas_call(
        add_kernel,
        in_specs=[VM],
        out_specs=VM,
        out_shape=jax.ShapeDtypeStruct((32, 4 * PAD, LANES), bf16),
        compiler_params=params(8),
        name="add_up",
    )(got)


def expert_kernel(got_ref, gate_ref, up_ref, down_ref, send_ref, rows):
    for s in range(SLOTS):
        for t in range(TILES):
            block = got_ref[s * TILES + t].astype(f32)
            for z in range(4):
                at = (z * TILES + t) * LANES
                rows[s * PAD:(s + 1) * PAD, at:at + LANES] = block[z * PAD:(z + 1) * PAD]
    slot_in = rows[...].astype(bf16)
    gate = lax.dot_general(slot_in, gate_ref[0], NT, preferred_element_type=f32)
    up = lax.dot_general(slot_in, up_ref[0], NT, preferred_element_type=f32)
    hidden = (gate / (1.0 + jnp.exp(-gate)) * up).astype(bf16)
    out = jnp.dot(hidden, down_ref[0], preferred_element_type=f32)
    for s in range(SLOTS):
        for t in range(TILES):
            block = jnp.concatenate(
                [
                    out[s * PAD:(s + 1) * PAD, (z * TILES + t) * LANES:(z * TILES + t + 1) * LANES]
                    for z in range(4)
                ]
            )
            send_ref[pl.ds((s * TILES + t) * 4 * PAD, 4 * PAD), :] = block.astype(bf16)


def expert(got, w_gate, w_up, w_down):
    return pl.pallas_call(
        expert_kernel,
        in_specs=[VM] * 4,
        out_specs=VM,
        out_shape=jax.ShapeDtypeStruct((SLOTS * TILES * 4 * PAD, LANES), bf16),
        scratch_shapes=[pltpu.VMEM((SLOTS * PAD, FULL), f32)],
        compiler_params=params(24),
        name="expert",
    )(got, w_gate, w_up, w_down)


def mix_kernel(got_ref, combine_ref, out_ref, slots, turned, block, left):
    for s in range(SLOTS):
        for t in range(TILES):
            slots[s * 32:(s + 1) * 32, t * LANES:(t + 1) * LANES] = got_ref[s * TILES + t]
    turned[...] = combine_ref[...].astype(f32).T
    lane = lax.broadcasted_iota(jnp.int32, (CHUNK, WS * PAD), 1) % PAD
    copies = []
    for g in range(GROUPS):
        for c in range(TOK // CHUNK):
            rows = pl.ds(c * CHUNK, CHUNK)
            mine = jnp.where(lane == g, turned[rows, :], 0.0).astype(bf16)
            block[g, rows, :] = jnp.dot(mine, slots[...], preferred_element_type=f32).astype(bf16)
            copy = pltpu.make_async_copy(
                block.at[g, rows], out_ref.at[g, rows], left.at[len(copies)]
            )
            copy.start()
            copies.append(copy)
    for copy in copies:
        copy.wait()


def mix(got, combine):
    return pl.pallas_call(
        mix_kernel,
        in_specs=[VM, VM],
        out_specs=HBM,
        out_shape=jax.ShapeDtypeStruct((GROUPS, TOK, WIDTH), bf16),
        scratch_shapes=[
            pltpu.VMEM((WS * PAD, WIDTH), bf16),
            pltpu.VMEM((TOK, WS * PAD), f32),
            pltpu.VMEM((GROUPS, TOK, WIDTH), bf16),
            pltpu.SemaphoreType.DMA((GROUPS * TOK // CHUNK,)),
        ],
        compiler_params=params(24),
        name="mix",
    )(got, combine)


def everyone(x):
    x = x.reshape(128, PAD, LANES)
    x = lax.all_to_all(x, ("dp", "tensor"), 0, 0, tiled=True)
    return x.reshape(128 * PAD, LANES)


def per_device(tokens, router, w_gate, w_up, w_down):
    first, second, held_a, held_b = partial_logits(tokens, router)
    near = lambda x: lax.ppermute(x, "tensor", [(i, i ^ 1) for i in range(4)])
    far = lambda x: lax.ppermute(x, "tensor", [(i, i ^ 3) for i in range(4)])
    first = first + near(first)
    second = second + far(second)
    parts = [first, far(first), second, near(second)]
    send, combine, log_total = dispatch(parts, (held_a, held_b))
    spread = merge(everyone(send))
    slot_in = lax.all_to_all(spread, "dp", 0, 0, tiled=True)
    outs = expert(slot_in, w_gate, w_up, w_down)
    spread = add_up(everyone(outs))
    slot_out = lax.all_to_all(spread, "dp", 0, 0, tiled=True)
    return (mix(slot_out, combine), log_total)


def solution(mesh):
    in_specs = (
        P(None, "dp", "tensor"),
        P(None, "tensor"),
        P("tensor", "dp", None),
        P("tensor", "dp", None),
        P("tensor", "dp", None),
    )
    out_specs = (P(None, "dp", "tensor"), P(None, "dp"))
    return jax.shard_map(
        per_device, mesh=mesh, in_specs=in_specs, out_specs=out_specs, check_vma=False
    )
```

```python
import functools

import jax
import jax.numpy as jnp
from jax import lax
from jax.experimental import pallas as pl
from jax.experimental.pallas import tpu as pltpu
from jax.sharding import PartitionSpec as P

GROUPS = 6
SLOTS = 4
EXPERTS = 4
WS = SLOTS * EXPERTS
PAD = 8
LANES = 128
TILES = 8
TOK = 512
WIDTH = TILES * LANES
FULL = 4096
HID = 448
HALF = GROUPS // 2
AROWS = HALF * WS + PAD
BROWS = HALF * WS
PIECE = 4 * GROUPS

CHUNK = 256

epsilon = 1e-05
bf16 = jnp.bfloat16
f32 = jnp.float32
NT = (((1,), (1,)), ((), ()))
VM = pl.BlockSpec(memory_space=pltpu.VMEM)
HBM = pl.BlockSpec(memory_space=pltpu.HBM)


def params(mib):
    return pltpu.CompilerParams(vmem_limit_bytes=mib << 20)


def logits_kernel(tokens_ref, router_ref, first_ref, second_ref, held_a, held_b, router, arrived):
    held = [(held_a, held_b)[g // HALF].at[g % HALF] for g in range(GROUPS)]
    fetch = pltpu.make_async_copy(router_ref, router, arrived.at[GROUPS])
    fetch.start()
    copies = [
        pltpu.make_async_copy(tokens_ref.at[g], held[g], arrived.at[g]) for g in range(GROUPS)
    ]
    for copy in copies:
        copy.start()
    first_ref[BROWS:, :] = jnp.zeros((PAD, TOK), f32)
    fetch.wait()
    for g in range(GROUPS):
        out_ref, h = (first_ref, second_ref)[g // HALF], g % HALF
        copies[g].wait()
        tok = held[g][...]
        out_ref[h * WS:(h + 1) * WS, :] = lax.dot_general(
            router[...], tok, NT, preferred_element_type=f32
        )
        total = jnp.zeros((TOK, LANES), f32)
        for t in range(TILES):
            part = tok[:, t * LANES:(t + 1) * LANES].astype(f32)
            total += part * part
        first_ref[BROWS + g:BROWS + g + 1, :] = jnp.sum(total.T, axis=0, keepdims=True)


def partial_logits(tokens, router):
    first = pltpu.VMEM((AROWS, TOK), f32)
    second = pltpu.VMEM((BROWS, TOK), f32)
    held = pltpu.VMEM((HALF, TOK, WIDTH), tokens.dtype)
    tokens = pltpu.with_memory_space_constraint(tokens, pltpu.HBM)
    router = pltpu.with_memory_space_constraint(router, pltpu.HBM)
    return pl.pallas_call(
        logits_kernel,
        in_specs=[HBM, HBM],
        out_specs=[VM] * 4,
        out_shape=[first, second, held, held],
        scratch_shapes=[
            pltpu.VMEM(router.shape, router.dtype),
            pltpu.SemaphoreType.DMA((GROUPS + 1,)),
        ],
        compiler_params=params(54),
        name="partial_logits",
    )(tokens, router)


def split3(value):
    high = value.astype(bf16).astype(f32)
    rest = value - high
    mid = rest.astype(bf16).astype(f32)
    return high, mid, rest - mid


def sum_logits(parts):
    first = parts[0][...] + parts[1][...]
    second = parts[2][...] + parts[3][...]
    scale = lax.rsqrt(first[BROWS:] * (1.0 / FULL) + epsilon)
    for g in range(GROUPS):
        half, h = divmod(g, HALF)
        norm = scale[g:g + 1]
        yield g, norm, (first, second)[half][h * WS:(h + 1) * WS] * norm


def dispatch_kernel(*refs):
    parts, (held_a, held_b, send_ref, combine_ref, log_ref, wts, peaks, sums, columns) = refs[:4], refs[4:]
    wts[...] = jnp.zeros_like(wts)
    peaks[...] = jnp.zeros_like(peaks)
    sums[...] = jnp.zeros_like(sums)
    columns[...] = jnp.zeros_like(columns)
    for g, norm, logits in sum_logits(parts):
        rows = pl.ds(g, WS, stride=PAD)
        peak = jnp.max(logits, axis=1, keepdims=True)
        powers = jnp.exp(logits - peak)
        weights = powers * norm
        for n in range(TOK // LANES):
            wts[n, rows, :] = weights[:, n * LANES:(n + 1) * LANES]
        peaks[rows, :] = jnp.broadcast_to(peak, (WS, LANES))
        sums[rows, :] = jnp.broadcast_to(jnp.sum(powers, axis=1, keepdims=True), (WS, LANES))
    weights = jnp.concatenate([wts[n] for n in range(TOK // LANES)], axis=1).astype(bf16)
    group = lax.broadcasted_iota(jnp.int32, (WS * PAD, TOK), 0) % PAD
    acc = jnp.zeros((WS * PAD, WIDTH), f32)
    for g in range(GROUPS):
        mine = jnp.where(group == g, weights, jnp.zeros_like(weights))
        held = (held_a, held_b)[g // HALF]
        acc += jnp.dot(mine, held[g % HALF], preferred_element_type=f32)
    lane = lax.broadcasted_iota(jnp.int32, (WS * PAD, LANES), 1)
    member = lax.broadcasted_iota(jnp.int32, (WS * PAD, LANES), 0) % PAD
    meta = jnp.zeros((WS * PAD, LANES), f32)
    for n, value in enumerate(split3(peaks[...]) + split3(sums[...])):
        meta += jnp.where(lane == member + n * PAD, value, 0.0)
    meta = jnp.sum(meta.reshape(WS, PAD, LANES), axis=1, keepdims=True)
    meta = jnp.broadcast_to(meta, (WS, PAD, LANES)).reshape(WS * PAD, LANES)
    for t in range(TILES):
        tile = jnp.where(member == GROUPS, meta, acc[:, t * LANES:(t + 1) * LANES])
        for s in range(SLOTS):
            block = jnp.concatenate(
                [tile[(4 * k + s) * PAD:(4 * k + s + 1) * PAD] for k in range(EXPERTS)]
            )
            send_ref[pl.ds((s * TILES + t) * EXPERTS * PAD, EXPERTS * PAD), :] = block.astype(bf16)

    for g, _, logits in sum_logits(parts):
        row_peak = jnp.max(logits, axis=0, keepdims=True)
        row_powers = jnp.exp(logits - row_peak)
        row_sum = jnp.sum(row_powers, axis=0, keepdims=True)
        combine = row_powers / row_sum
        log_ref[g:g + 1, :] = row_peak + jnp.log(row_sum)
        for n in range(TOK // LANES):
            for k in range(EXPERTS):
                rows = pl.ds(k * GROUPS + g, SLOTS, stride=PIECE)
                columns[g % 2, n, rows, :] = combine[k * SLOTS:(k + 1) * SLOTS, n * LANES:(n + 1) * LANES]
            combine_ref[g, n * LANES:(n + 1) * LANES, :] = columns[g % 2, n].T.astype(bf16)
            for k in range(EXPERTS):
                rows = pl.ds(k * GROUPS + g, SLOTS, stride=PIECE)
                columns[g % 2, n, rows, :] = jnp.zeros((SLOTS, LANES), f32)


def dispatch(parts, held):
    return pl.pallas_call(
        dispatch_kernel,
        in_specs=[VM] * 6,
        out_specs=[VM] * 3,
        out_shape=[
            jax.ShapeDtypeStruct((SLOTS * TILES * EXPERTS * PAD, LANES), bf16),
            jax.ShapeDtypeStruct((GROUPS, TOK, LANES), bf16),
            jax.ShapeDtypeStruct((GROUPS, TOK), f32),
        ],
        scratch_shapes=[
            pltpu.VMEM((TOK // LANES, WS * PAD, LANES), f32),
            pltpu.VMEM((WS * PAD, LANES), f32),
            pltpu.VMEM((WS * PAD, LANES), f32),
            pltpu.VMEM((2, TOK // LANES, LANES, LANES), f32),
        ],
        compiler_params=params(20),
        name="dispatch",
    )(*parts, *held)


def merge_kernel(got_ref, out_ref, wide):
    wide[...] = got_ref[...].astype(f32)
    meta = wide[pl.ds(GROUPS, 32, stride=EXPERTS * PAD), :]
    shift = lambda n: pltpu.roll(meta, (LANES - n * PAD) % LANES, 1)
    lane = lax.broadcasted_iota(jnp.int32, (32, LANES), 1)
    peak = (meta + shift(1)) + shift(2)
    local = (shift(3) + shift(4)) + shift(5)
    peak = jnp.where(lane < GROUPS, peak, 0.0)
    factor = jnp.exp(peak - jnp.max(peak, axis=0, keepdims=True))
    total = jnp.sum(factor * local, axis=0, keepdims=True)
    factor = jnp.where(lane < GROUPS, factor / jnp.where(lane[0:1] < GROUPS, total, 1.0), 0.0)
    square = jnp.concatenate([factor, jnp.zeros((LANES - 32, LANES), f32)])
    columns = square.T[0:PAD]
    acc = [jnp.zeros((PAD, LANES), f32) for _ in range(4)]
    for i in range(32):
        by = jnp.broadcast_to(columns[:, i:i + 1], (PAD, LANES))
        for z in range(4):
            row = (i * 4 + z) * PAD
            acc[z] += by * wide[row:row + PAD, :]
    block = jnp.concatenate([part[:GROUPS] for part in acc]).astype(bf16)
    for i in range(32):
        out_ref[i] = block


def add_kernel(got_ref, out_ref):
    rows = 4 * PAD
    acc = got_ref[0:rows, :].astype(f32)
    for i in range(1, 32):
        acc += got_ref[i * rows:(i + 1) * rows, :].astype(f32)
    block = jnp.concatenate([acc[k * PAD:k * PAD + GROUPS] for k in range(4)]).astype(bf16)
    for i in range(32):
        out_ref[i] = block


def merge(got):
    return pl.pallas_call(
        merge_kernel,
        in_specs=[VM],
        out_specs=VM,
        out_shape=jax.ShapeDtypeStruct((32, PIECE, LANES), bf16),
        scratch_shapes=[pltpu.VMEM((32 * 4 * PAD, LANES), f32)],
        compiler_params=params(8),
        name="merge",
    )(got)


def add_up(got):
    return pl.pallas_call(
        add_kernel,
        in_specs=[VM],
        out_specs=VM,
        out_shape=jax.ShapeDtypeStruct((32, PIECE, LANES), bf16),
        compiler_params=params(8),
        name="add_up",
    )(got)


def expert_kernel(got_ref, gate_ref, up_ref, down_ref, send_ref, rows):
    rows[...] = jnp.zeros_like(rows)
    for s in range(SLOTS):
        for t in range(TILES):
            block = got_ref[s * TILES + t].astype(f32)
            for z in range(4):
                at = (z * TILES + t) * LANES
                rows[s * PAD:s * PAD + GROUPS, at:at + LANES] = block[z * GROUPS:(z + 1) * GROUPS]
    slot_in = rows[...].astype(bf16)
    gate = lax.dot_general(slot_in, gate_ref[0], NT, preferred_element_type=f32)
    up = lax.dot_general(slot_in, up_ref[0], NT, preferred_element_type=f32)
    hidden = (gate / (1.0 + jnp.exp(-gate)) * up).astype(bf16)
    out = jnp.dot(hidden, down_ref[0], preferred_element_type=f32)
    for s in range(SLOTS):
        for t in range(TILES):
            block = jnp.concatenate(
                [
                    out[s * PAD:(s + 1) * PAD, (z * TILES + t) * LANES:(z * TILES + t + 1) * LANES]
                    for z in range(4)
                ]
            )
            send_ref[pl.ds((s * TILES + t) * 4 * PAD, 4 * PAD), :] = block.astype(bf16)


def expert(got, w_gate, w_up, w_down):
    return pl.pallas_call(
        expert_kernel,
        in_specs=[VM] * 4,
        out_specs=VM,
        out_shape=jax.ShapeDtypeStruct((SLOTS * TILES * 4 * PAD, LANES), bf16),
        scratch_shapes=[pltpu.VMEM((SLOTS * PAD, FULL), f32)],
        compiler_params=params(24),
        name="expert",
    )(got, w_gate, w_up, w_down)


def mix_kernel(got_ref, combine_ref, out_ref, rows, slots, block, left):
    rows[SLOTS * PIECE:, :] = jnp.zeros((LANES - SLOTS * PIECE, WIDTH), f32)
    for s in range(SLOTS):
        for t in range(TILES):
            rows[s * PIECE:(s + 1) * PIECE, t * LANES:(t + 1) * LANES] = got_ref[s * TILES + t].astype(f32)
    slots[...] = rows[...].astype(bf16)
    copies = []
    for g in range(GROUPS):
        for c in range(TOK // CHUNK):
            part = pl.ds(c * CHUNK, CHUNK)
            mixed = jnp.dot(combine_ref[g, part, :], slots[...], preferred_element_type=f32)
            block[g, part, :] = mixed.astype(bf16)
            copy = pltpu.make_async_copy(
                block.at[g, part], out_ref.at[g, part], left.at[len(copies)]
            )
            copy.start()
            copies.append(copy)
    for copy in copies:
        copy.wait()


def mix(got, combine):
    return pl.pallas_call(
        mix_kernel,
        in_specs=[VM, VM],
        out_specs=HBM,
        out_shape=jax.ShapeDtypeStruct((GROUPS, TOK, WIDTH), bf16),
        scratch_shapes=[
            pltpu.VMEM((LANES, WIDTH), f32),
            pltpu.VMEM((LANES, WIDTH), bf16),
            pltpu.VMEM((GROUPS, TOK, WIDTH), bf16),
            pltpu.SemaphoreType.DMA((GROUPS * TOK // CHUNK,)),
        ],
        compiler_params=params(24),
        name="mix",
    )(got, combine)


def everyone(x):
    x = x.reshape(128, PAD, LANES)
    x = lax.all_to_all(x, ("dp", "tensor"), 0, 0, tiled=True)
    return x.reshape(128 * PAD, LANES)


def per_device(tokens, router, w_gate, w_up, w_down):
    first, second, held_a, held_b = partial_logits(tokens, router)
    near = lambda x: lax.ppermute(x, "tensor", [(i, i ^ 1) for i in range(4)])
    far = lambda x: lax.ppermute(x, "tensor", [(i, i ^ 3) for i in range(4)])
    first = first + near(first)
    second = second + far(second)
    parts = [first, far(first), second, near(second)]
    send, combine, log_total = dispatch(parts, (held_a, held_b))
    spread = merge(everyone(send))
    slot_in = lax.all_to_all(spread, "dp", 0, 0, tiled=True)
    outs = expert(slot_in, w_gate, w_up, w_down)
    spread = add_up(everyone(outs))
    slot_out = lax.all_to_all(spread, "dp", 0, 0, tiled=True)
    return (mix(slot_out, combine), log_total)


def solution(mesh):
    in_specs = (
        P(None, "dp", "tensor"),
        P(None, "tensor"),
        P("tensor", "dp", None),
        P("tensor", "dp", None),
        P("tensor", "dp", None),
    )
    out_specs = (P(None, "dp", "tensor"), P(None, "dp"))
    return jax.shard_map(
        per_device, mesh=mesh, in_specs=in_specs, out_specs=out_specs, check_vma=False
    )
```

```python
import functools

import jax
import jax.numpy as jnp
from jax import lax
from jax.experimental import pallas as pl
from jax.experimental.pallas import tpu as pltpu
from jax.sharding import PartitionSpec as P

GROUPS = 6
SLOTS = 4
EXPERTS = 4
WS = SLOTS * EXPERTS
PAD = 8
LANES = 128
TILES = 8
TOK = 512
WIDTH = TILES * LANES
FULL = 4096
HID = 448
HALF = GROUPS // 2
AROWS = HALF * WS + PAD
BROWS = HALF * WS
PIECE = 4 * GROUPS

CHUNK = 256
SPLIT = 1
SPAN = TOK // SPLIT

epsilon = 1e-05
bf16 = jnp.bfloat16
f32 = jnp.float32
NT = (((1,), (1,)), ((), ()))
TN = (((0,), (0,)), ((), ()))
VM = pl.BlockSpec(memory_space=pltpu.VMEM)
HBM = pl.BlockSpec(memory_space=pltpu.HBM)


def params(mib):
    return pltpu.CompilerParams(vmem_limit_bytes=mib << 20)


def logits_kernel(tokens_ref, router_ref, first_ref, second_ref, held_a, held_b, router, arrived):
    held = [(held_a, held_b)[g // HALF].at[g % HALF] for g in range(GROUPS)]
    fetch = pltpu.make_async_copy(router_ref, router, arrived.at[GROUPS * SPLIT])
    fetch.start()
    copies = []
    for g in range(GROUPS):
        for c in range(SPLIT):
            part = pl.ds(c * SPAN, SPAN)
            copies.append(
                pltpu.make_async_copy(
                    tokens_ref.at[g, part], held[g].at[part], arrived.at[g * SPLIT + c]
                )
            )
    for copy in copies:
        copy.start()
    first_ref[BROWS:, :] = jnp.zeros((PAD, TOK), f32)
    row = lax.broadcasted_iota(jnp.int32, (WS, WS), 0)
    column = lax.broadcasted_iota(jnp.int32, (WS, WS), 1)
    swap = (column == (row % EXPERTS) * SLOTS + row // EXPERTS).astype(f32).astype(bf16)
    fetch.wait()
    slots = jnp.dot(swap, router[...], preferred_element_type=f32).astype(bf16)
    for g in range(GROUPS):
        out_ref, h = (first_ref, second_ref)[g // HALF], g % HALF
        for c in range(SPLIT):
            copies[g * SPLIT + c].wait()
            part = slice(c * SPAN, (c + 1) * SPAN)
            tok = held[g][part, :]
            out_ref[h * WS:(h + 1) * WS, part] = lax.dot_general(
                slots, tok, NT, preferred_element_type=f32
            )
            total = jnp.zeros((SPAN, LANES), f32)
            for t in range(TILES):
                piece = tok[:, t * LANES:(t + 1) * LANES].astype(f32)
                total += piece * piece
            first_ref[BROWS + g:BROWS + g + 1, part] = jnp.sum(total.T, axis=0, keepdims=True)


def partial_logits(tokens, router):
    first = pltpu.VMEM((AROWS, TOK), f32)
    second = pltpu.VMEM((BROWS, TOK), f32)
    held = pltpu.VMEM((HALF, TOK, WIDTH), tokens.dtype)
    tokens = pltpu.with_memory_space_constraint(tokens, pltpu.HBM)
    router = pltpu.with_memory_space_constraint(router, pltpu.HBM)
    return pl.pallas_call(
        logits_kernel,
        in_specs=[HBM, HBM],
        out_specs=[VM] * 4,
        out_shape=[first, second, held, held],
        scratch_shapes=[
            pltpu.VMEM(router.shape, router.dtype),
            pltpu.SemaphoreType.DMA((GROUPS * SPLIT + 1,)),
        ],
        compiler_params=params(54),
        name="partial_logits",
    )(tokens, router)


def split3(value):
    high = value.astype(bf16).astype(f32)
    rest = value - high
    mid = rest.astype(bf16).astype(f32)
    return high, mid, rest - mid


def scaled_logits(parts):
    first = parts[0][...] + parts[1][...]
    second = parts[2][...] + parts[3][...]
    scale = lax.rsqrt(first[BROWS:] * (1.0 / FULL) + epsilon)
    for half, total in enumerate((first, second)):
        norm = scale[half * HALF:(half + 1) * HALF][:, None, :]
        yield half, norm, total[:BROWS].reshape(HALF, WS, TOK) * norm


def dispatch_kernel(*refs):
    parts, (held_a, held_b, send_ref, combine_ref, log_ref, wts, peaks, sums) = refs[:4], refs[4:]
    wts[...] = jnp.zeros_like(wts)
    peaks[...] = jnp.zeros_like(peaks)
    sums[...] = jnp.zeros_like(sums)
    for half, norm, logits in scaled_logits(parts):
        peak = jnp.max(logits, axis=2, keepdims=True)
        row_peak = jnp.max(logits, axis=1, keepdims=True)
        powers = jnp.exp(logits - peak)
        row_powers = jnp.exp(logits - row_peak)
        total = jnp.sum(powers, axis=2, keepdims=True)
        row_sum = jnp.sum(row_powers, axis=1, keepdims=True)
        weights = powers * norm
        combine = (row_powers * (1.0 / row_sum)).astype(bf16)
        log_total = row_peak + jnp.log(row_sum)
        for h in range(HALF):
            g = half * HALF + h
            rows = pl.ds(g, WS, stride=PAD)
            for n in range(TOK // LANES):
                wts[n, rows, :] = weights[h, :, n * LANES:(n + 1) * LANES]
            peaks[rows, :] = jnp.broadcast_to(peak[h], (WS, LANES))
            sums[rows, :] = jnp.broadcast_to(total[h], (WS, LANES))
            combine_ref[g] = combine[h]
            log_ref[g:g + 1, :] = log_total[h]
    weights = jnp.concatenate([wts[n] for n in range(TOK // LANES)], axis=1).astype(bf16)
    group = lax.broadcasted_iota(jnp.int32, (WS * PAD, TOK), 0) % PAD
    acc = jnp.zeros((WS * PAD, WIDTH), f32)
    for g in range(GROUPS):
        mine = jnp.where(group == g, weights, jnp.zeros_like(weights))
        held = (held_a, held_b)[g // HALF]
        acc += jnp.dot(mine, held[g % HALF], preferred_element_type=f32)
    lane = lax.broadcasted_iota(jnp.int32, (WS * PAD, LANES), 1)
    member = lax.broadcasted_iota(jnp.int32, (WS * PAD, LANES), 0) % PAD
    meta = jnp.zeros((WS * PAD, LANES), f32)
    for n, value in enumerate(split3(peaks[...]) + split3(sums[...])):
        meta += jnp.where(lane == member + n * PAD, value, 0.0)
    meta = jnp.sum(meta.reshape(WS, PAD, LANES), axis=1, keepdims=True)
    meta = jnp.broadcast_to(meta, (WS, PAD, LANES)).reshape(WS * PAD, LANES)
    for t in range(TILES):
        tile = jnp.where(member == GROUPS, meta, acc[:, t * LANES:(t + 1) * LANES])
        for s in range(SLOTS):
            block = tile[s * EXPERTS * PAD:(s + 1) * EXPERTS * PAD]
            send_ref[pl.ds((s * TILES + t) * EXPERTS * PAD, EXPERTS * PAD), :] = block.astype(bf16)


def dispatch(parts, held):
    return pl.pallas_call(
        dispatch_kernel,
        in_specs=[VM] * 6,
        out_specs=[VM] * 3,
        out_shape=[
            jax.ShapeDtypeStruct((SLOTS * TILES * EXPERTS * PAD, LANES), bf16),
            jax.ShapeDtypeStruct((GROUPS, WS, TOK), bf16),
            jax.ShapeDtypeStruct((GROUPS, TOK), f32),
        ],
        scratch_shapes=[
            pltpu.VMEM((TOK // LANES, WS * PAD, LANES), f32),
            pltpu.VMEM((WS * PAD, LANES), f32),
            pltpu.VMEM((WS * PAD, LANES), f32),
        ],
        compiler_params=params(20),
        name="dispatch",
    )(*parts, *held)


def merge_kernel(got_ref, out_ref, wide):
    wide[...] = got_ref[...].astype(f32)
    meta = wide[pl.ds(GROUPS, 32, stride=EXPERTS * PAD), :]
    shift = lambda n: pltpu.roll(meta, (LANES - n * PAD) % LANES, 1)
    lane = lax.broadcasted_iota(jnp.int32, (32, LANES), 1)
    peak = (meta + shift(1)) + shift(2)
    local = (shift(3) + shift(4)) + shift(5)
    peak = jnp.where(lane < GROUPS, peak, 0.0)
    factor = jnp.exp(peak - jnp.max(peak, axis=0, keepdims=True))
    total = jnp.sum(factor * local, axis=0, keepdims=True)
    factor = jnp.where(lane < GROUPS, factor / jnp.where(lane[0:1] < GROUPS, total, 1.0), 0.0)
    square = jnp.concatenate([factor, jnp.zeros((LANES - 32, LANES), f32)])
    columns = square.T[0:PAD]
    acc = [jnp.zeros((PAD, LANES), f32) for _ in range(4)]
    for i in range(32):
        by = jnp.broadcast_to(columns[:, i:i + 1], (PAD, LANES))
        for z in range(4):
            row = (i * 4 + z) * PAD
            acc[z] += by * wide[row:row + PAD, :]
    block = jnp.concatenate([part[:GROUPS] for part in acc]).astype(bf16)
    for i in range(32):
        out_ref[i] = block


def add_kernel(got_ref, out_ref, mixed):
    rows = 4 * PAD
    acc = got_ref[0:rows, :].astype(f32)
    for i in range(1, 32):
        acc += got_ref[i * rows:(i + 1) * rows, :].astype(f32)
    for k in range(EXPERTS):
        mixed[pl.ds(k, PAD, stride=EXPERTS), :] = acc[k * PAD:(k + 1) * PAD]
    block = mixed[:PIECE, :].astype(bf16)
    for i in range(32):
        out_ref[i] = block


def merge(got):
    return pl.pallas_call(
        merge_kernel,
        in_specs=[VM],
        out_specs=VM,
        out_shape=jax.ShapeDtypeStruct((32, PIECE, LANES), bf16),
        scratch_shapes=[pltpu.VMEM((32 * 4 * PAD, LANES), f32)],
        compiler_params=params(8),
        name="merge",
    )(got)


def add_up(got):
    return pl.pallas_call(
        add_kernel,
        in_specs=[VM],
        out_specs=VM,
        out_shape=jax.ShapeDtypeStruct((32, PIECE, LANES), bf16),
        scratch_shapes=[pltpu.VMEM((EXPERTS * PAD, LANES), f32)],
        compiler_params=params(8),
        name="add_up",
    )(got)


def expert_kernel(got_ref, gate_ref, up_ref, down_ref, send_ref, rows):
    rows[...] = jnp.zeros_like(rows)
    for s in range(SLOTS):
        for t in range(TILES):
            block = got_ref[s * TILES + t].astype(f32)
            for z in range(4):
                at = (z * TILES + t) * LANES
                rows[s * PAD:s * PAD + GROUPS, at:at + LANES] = block[z * GROUPS:(z + 1) * GROUPS]
    slot_in = rows[...].astype(bf16)
    gate = lax.dot_general(slot_in, gate_ref[0], NT, preferred_element_type=f32)
    up = lax.dot_general(slot_in, up_ref[0], NT, preferred_element_type=f32)
    hidden = (gate / (1.0 + jnp.exp(-gate)) * up).astype(bf16)
    out = jnp.dot(hidden, down_ref[0], preferred_element_type=f32)
    for s in range(SLOTS):
        for t in range(TILES):
            block = jnp.concatenate(
                [
                    out[s * PAD:(s + 1) * PAD, (z * TILES + t) * LANES:(z * TILES + t + 1) * LANES]
                    for z in range(4)
                ]
            )
            send_ref[pl.ds((s * TILES + t) * 4 * PAD, 4 * PAD), :] = block.astype(bf16)


def expert(got, w_gate, w_up, w_down):
    return pl.pallas_call(
        expert_kernel,
        in_specs=[VM] * 4,
        out_specs=VM,
        out_shape=jax.ShapeDtypeStruct((SLOTS * TILES * 4 * PAD, LANES), bf16),
        scratch_shapes=[pltpu.VMEM((SLOTS * PAD, FULL), f32)],
        compiler_params=params(24),
        name="expert",
    )(got, w_gate, w_up, w_down)


def mix_kernel(got_ref, combine_ref, log_ref, out_ref, log_out, rows, block, left):
    copies = [pltpu.make_async_copy(log_ref, log_out, left.at[0])]
    copies[0].start()
    for s in range(SLOTS):
        for t in range(TILES):
            piece = got_ref[s * TILES + t].astype(f32)
            for g in range(GROUPS):
                rows[g, s * EXPERTS:(s + 1) * EXPERTS, t * LANES:(t + 1) * LANES] = piece[
                    g * EXPERTS:(g + 1) * EXPERTS
                ]
    for g in range(GROUPS):
        slots = rows[g].astype(bf16)
        for c in range(TOK // CHUNK):
            part = pl.ds(c * CHUNK, CHUNK)
            mixed = lax.dot_general(
                combine_ref[g, :, part], slots, TN, preferred_element_type=f32
            )
            block[g, part, :] = mixed.astype(bf16)
            copy = pltpu.make_async_copy(
                block.at[g, part], out_ref.at[g, part], left.at[len(copies)]
            )
            copy.start()
            copies.append(copy)
    for copy in copies:
        copy.wait()


def mix(got, combine, log_total):
    return pl.pallas_call(
        mix_kernel,
        in_specs=[VM] * 3,
        out_specs=[HBM] * 2,
        out_shape=[
            jax.ShapeDtypeStruct((GROUPS, TOK, WIDTH), bf16),
            jax.ShapeDtypeStruct((GROUPS, TOK), f32),
        ],
        scratch_shapes=[
            pltpu.VMEM((GROUPS, WS, WIDTH), f32),
            pltpu.VMEM((GROUPS, TOK, WIDTH), bf16),
            pltpu.SemaphoreType.DMA((1 + GROUPS * TOK // CHUNK,)),
        ],
        compiler_params=params(24),
        name="mix",
    )(got, combine, log_total)


def everyone(x):
    x = x.reshape(128, PAD, LANES)
    x = lax.all_to_all(x, ("dp", "tensor"), 0, 0, tiled=True)
    return x.reshape(128 * PAD, LANES)


def per_device(tokens, router, w_gate, w_up, w_down):
    first, second, held_a, held_b = partial_logits(tokens, router)
    near = lambda x: lax.ppermute(x, "tensor", [(i, i ^ 1) for i in range(4)])
    far = lambda x: lax.ppermute(x, "tensor", [(i, i ^ 3) for i in range(4)])
    first = first + near(first)
    second = second + far(second)
    parts = [first, far(first), second, near(second)]
    send, combine, log_total = dispatch(parts, (held_a, held_b))
    spread = merge(everyone(send))
    slot_in = lax.all_to_all(spread, "dp", 0, 0, tiled=True)
    outs = expert(slot_in, w_gate, w_up, w_down)
    spread = add_up(everyone(outs))
    slot_out = lax.all_to_all(spread, "dp", 0, 0, tiled=True)
    return tuple(mix(slot_out, combine, log_total))


def solution(mesh):
    in_specs = (
        P(None, "dp", "tensor"),
        P(None, "tensor"),
        P("tensor", "dp", None),
        P("tensor", "dp", None),
        P("tensor", "dp", None),
    )
    out_specs = (P(None, "dp", "tensor"), P(None, "dp"))
    return jax.shard_map(
        per_device, mesh=mesh, in_specs=in_specs, out_specs=out_specs, check_vma=False
    )
```
